256 devices in a mesh: slab: 8 (over y, core), tile: 32 (over x, z).
Axes of the slice: x: 4, y: 4, z: 8, core: 2. Of those that a mesh axis runs over, the one named last changes fastest.
Arguments:
- local_field: float32 [2, 64, 8, 49152], P(None, None, 'slab', 'tile'), may hold values from -6 to 6
- material: int32 [8, 49152], P('slab', 'tile'), may hold values from 0 to 15
- contrast: float32 [16], replicated, may hold values from 0.5 to 1.2
- low_left: float32 [8, 2, 256, 49152], P('slab', None, None, 'tile'), may hold values from -0.21875 to 0.21875
- low_right: float32 [8, 2, 49152, 256], P('slab', None, 'tile'), may hold values from -0.02734375 to 0.02734375
- near_blocks: float32 [8, 2, 384, 384, 128], P('slab', None, 'tile'), may hold values from -0.21875 to 0.21875
Outputs:
- traces: float32 [2, 64, 8, 49152], P(None, None, 'slab', 'tile')
The draws below stay inside these ranges and needn't reach their ends.
All inputs are finite; a program needn't handle non-finite values.
Results may differ from the reference program's by a relative error of at most 0.00014.
Values sent between devices are 32-bit elements; how exact they have to be, the bound alone decides.
No kernel may reach another device: no remote copies, remote signals or barrier semaphores. Data moves between devices by JAX's collectives and lax.ppermute only.
A program may use at most 64 MiB of HBM per device.

```python
import math
import jax
import jax.numpy as jnp
from jax import lax

SRC = 64
RANK = 256
BLOCK = 128
MATS = 16
NPTS = 49152
INTERFACES = 8
NBLK = 384


def touch_ends(result, key, low, high):
    index_at = [jax.random.randint(jax.random.fold_in(key, axis), (), 0, length) for axis, length in enumerate(result.shape)]
    main_axis = result.shape.index(max(result.shape))
    beside = index_at[:main_axis] + [(index_at[main_axis] + 1) % result.shape[main_axis]] + index_at[main_axis + 1:]
    return result.at[tuple(index_at)].set(low).at[tuple(beside)].set(high)


def block_levels(key, extent, cuts, least, high):
    gain = 1.0
    for dim, shards_of in cuts:
        draws = jax.random.uniform(jax.random.fold_in(jax.random.fold_in(key, 6), dim), (shards_of,), jnp.float32, least / len(cuts), high / len(cuts))
        gain = gain * jnp.repeat(jnp.exp(draws), extent[dim] // shards_of).reshape((-1,) + (1,) * (len(extent) - 1 - dim))
    return gain


def centred(stream_key, shape, spread, limit, cuts=(), held_as=jnp.bfloat16):
    array = spread * jax.random.normal(stream_key, shape, jnp.float32)
    if cuts:
        array = array * block_levels(stream_key, shape, cuts, -0.22, 0.18)
    return jnp.clip(array, -limit, limit).astype(held_as)


def setup_inputs(seed: int = 0) -> dict:
    keys = jax.random.split(jax.random.key(seed), 7)
    local_field = centred(keys[0], (2, SRC, INTERFACES, NPTS), 1.0, 6.0, ((2, 8), (3, 32)), jnp.float32)
    material = touch_ends(jax.random.randint(keys[1], (INTERFACES, NPTS), 0, MATS), jax.random.fold_in(keys[1], 1), 0, MATS - 1).astype(jnp.int32)
    contrast = jnp.clip(jnp.exp(jax.random.uniform(keys[2], (MATS,), jnp.float32, math.log(0.5), math.log(1.2))), 0.5, 1.2)
    low_left = centred(keys[3], (INTERFACES, 2, RANK, NPTS), (3 * RANK) ** -0.5, 0.21875, ((0, 8), (3, 32)), jnp.float32)
    low_right = centred(keys[4], (INTERFACES, 2, NPTS, RANK), NPTS ** -0.5, 0.02734375, ((0, 8), (2, 32)), jnp.float32)
    near_blocks = centred(keys[5], (INTERFACES, 2, NBLK, 3 * BLOCK, BLOCK), (6 * BLOCK) ** -0.5, 0.21875, ((0, 8), (2, 32)), jnp.float32)
    return dict(local_field=local_field, material=material, contrast=contrast, low_left=low_left, low_right=low_right, near_blocks=near_blocks)


def complex_product(pattern, first, second):
    high = lax.Precision.HIGHEST
    real_part = jnp.einsum(pattern, first[0], second[0], precision=high) - jnp.einsum(pattern, first[1], second[1], precision=high)
    imag_part = jnp.einsum(pattern, first[0], second[1], precision=high) + jnp.einsum(pattern, first[1], second[0], precision=high)
    return jnp.stack([real_part, imag_part])


def near_product(extended, blocks, points):
    block_width = blocks.shape[-1]
    block_count = points // block_width
    sources = extended.shape[1]
    pieces = [extended[:, :, k * block_width:k * block_width + points].reshape(2, sources, block_count, block_width) for k in range(3)]
    windows = jnp.concatenate(pieces, axis=-1)
    return complex_product('sbk,bki->sbi', windows, blocks).reshape(2, sources, points)


def reference(local_field, material, contrast, low_left, low_right, near_blocks):
    previous = jnp.zeros((2, SRC, NPTS), jnp.float32)
    traces_list = []
    for interface in range(INTERFACES):
        factor = contrast[material[interface]]
        coefficients = complex_product('sp,pr->sr', previous, low_right[interface])
        far_part = complex_product('sr,rp->sp', coefficients, low_left[interface])
        extended = jnp.pad(previous, ((0, 0), (0, 0), (BLOCK, BLOCK)))
        close_part = near_product(extended, near_blocks[interface], NPTS)
        previous = local_field[:, :, interface] + factor * (far_part + close_part)
        traces_list.append(previous)
    return jnp.stack(traces_list, axis=2)
```

```python
import functools
import jax
import jax.numpy as jnp
from jax import lax
from jax.experimental import pallas as pl
from jax.experimental.pallas import tpu as pltpu
from jax.sharding import PartitionSpec as P

AXES = ("slab", "tile")
BLOCK = 128
PARAMS = pltpu.CompilerParams(vmem_limit_bytes=44 * 1024 * 1024)
SMEM = pl.BlockSpec(memory_space=pltpu.SMEM)


def halves(x):
    high = x.astype(jnp.bfloat16)
    low = (x - high.astype(jnp.float32)).astype(jnp.bfloat16)
    return high, low


def dot(a, b):
    return jnp.dot(a, b, preferred_element_type=jnp.float32)


def split_dot(high, low, w_high, w_low):
    rows = high.shape[0]
    both = dot(jnp.concatenate([high, low], axis=0), w_high)
    return both[:rows] + both[rows:] + dot(high, w_low)


def complex_dot(high, low, wr_high, wr_low, wi_high, wi_low):
    with_real = split_dot(high, low, wr_high, wr_low)
    with_imag = split_dot(high, low, wi_high, wi_low)
    half = with_real.shape[0] // 2
    return jnp.concatenate(
        [
            with_real[:half] - with_imag[half:],
            with_imag[:half] + with_real[half:],
        ],
        axis=0,
    )


def at_step(step, body):
    pl.when(pl.program_id(0) == step)(body)


def store_edges(steps, part, first_ref, last_ref):
    def store_first():
        first_ref[...] = part[:, :BLOCK]

    def store_last():
        last_ref[...] = part[:, -BLOCK:]

    at_step(0, store_first)
    at_step(steps - 1, store_last)


def right_kernel(steps, count, flags, *refs):
    xs, (rh_ref, rl_ref, p_ref, acc) = refs[:count], refs[count:]
    x = xs[0][...]
    if count == 2:
        x = jnp.where(flags[3] == 1, xs[1][...], jnp.where(flags[0] == 1, 0.0, x))
    high, low = halves(x)
    share = complex_dot(high, low, rh_ref[0], rl_ref[0], rh_ref[1], rl_ref[1])

    def start():
        acc[...] = share

    def finish():
        whole = acc[...]
        p_ref[0] = whole[:, :BLOCK].reshape(p_ref.shape[1:])
        p_ref[1] = whole[:, BLOCK:].reshape(p_ref.shape[1:])

    at_step(0, start)

    @pl.when(pl.program_id(0) > 0)
    def _():
        acc[...] += share

    at_step(steps - 1, finish)


def far_kernel(steps, count, pick, flags, *refs):
    coefs, refs = refs[:count], refs[count:]
    weights, refs = refs[: 2 * count], refs[2 * count :]
    bases, outs = (refs[:2], refs[2:]) if pick else (refs[:1], refs[1:])
    base = bases[0][...]
    if pick:
        base = jnp.where(flags[3] == 1, bases[1][...], base)
    total = base
    for k in range(count):
        c_ref, high_ref, low_ref = coefs[k], weights[2 * k], weights[2 * k + 1]
        c = jnp.concatenate([c_ref[0].reshape(-1, BLOCK), c_ref[1].reshape(-1, BLOCK)], axis=1)
        high, low = halves(c)
        more = complex_dot(high, low, high_ref[0], low_ref[0], high_ref[1], low_ref[1])
        if k == 1:
            more = jnp.where(flags[3] == 1, more, 0.0)
        total = total + more
    outs[0][...] = total
    if len(outs) > 1:
        store_edges(steps, total, *outs[1:])


def near_kernel(steps, group, own, edges, flags, x_ref, before_ref, after_ref, *refs):
    if own:
        l_ref, refs = refs[0], refs[1:]
    nh_ref, nl_ref, w_ref = refs[:3]
    high, low = refs[-2:]
    points = x_ref.shape[1]

    def load():
        before = jnp.where(flags[1] == 1, 0.0, before_ref[...])
        after = jnp.where(flags[2] == 1, 0.0, after_ref[...])
        high[:, :BLOCK], low[:, :BLOCK] = halves(before)
        high[:, BLOCK : BLOCK + points], low[:, BLOCK : BLOCK + points] = halves(x_ref[...])
        high[:, BLOCK + points :], low[:, BLOCK + points :] = halves(after)

    at_step(0, load)
    parts = []
    for k in range(group):
        start = pl.multiple_of((pl.program_id(0) * group + k) * BLOCK, BLOCK)
        window = pl.ds(start, 3 * BLOCK)
        both = split_dot(high[:, window], low[:, window], nh_ref[k], nl_ref[k])
        half = both.shape[0] // 2
        part = jnp.concatenate(
            [
                both[:half, :BLOCK] - both[half:, BLOCK:],
                both[:half, BLOCK:] + both[half:, :BLOCK],
            ],
            axis=0,
        )
        here = slice(k * BLOCK, (k + 1) * BLOCK)
        if own:
            mine = l_ref[:, here]
            part = jnp.where(flags[0] == 1, mine, mine + part)
        w_ref[:, here] = part
        parts.append(part)
    if edges:

        def store_first():
            refs[3][...] = parts[0]

        def store_last():
            refs[4][...] = parts[-1]

        at_step(0, store_first)
        at_step(steps - 1, store_last)


def scale_kernel(x_ref, factor_ref, high_ref, low_ref):
    high_ref[...], low_ref[...] = halves(x_ref[...] * factor_ref[...])


def split_kernel(x_ref, high_ref, low_ref):
    high_ref[...], low_ref[...] = halves(x_ref[...])


def pair_kernel(x_ref, factor_ref, high_ref, low_ref):
    for k in range(2):
        here = slice(k * BLOCK, (k + 1) * BLOCK)
        high_ref[:, :, here], low_ref[:, :, here] = halves(x_ref[k] * factor_ref[...])


def sum_kernel(parts_ref, copies_ref):
    copies_ref[...] = jnp.broadcast_to(jnp.sum(parts_ref[...], axis=0)[None], copies_ref.shape)


def f32(*shape):
    return jax.ShapeDtypeStruct(shape, jnp.float32)


def call(body, grid, args, ins, outs, out_shape, flops=0, scratch=()):
    size = sum(a.size * a.dtype.itemsize for a in args)
    return pl.pallas_call(
        body,
        grid=grid,
        in_specs=ins,
        out_specs=outs,
        out_shape=out_shape,
        scratch_shapes=scratch,
        compiler_params=PARAMS,
        cost_estimate=pl.CostEstimate(flops=flops, bytes_accessed=size, transcendentals=0),
    )(*args)


def fixed(*shape):
    return pl.BlockSpec(shape, lambda i: (0,) * len(shape))


def chunk_of(points):
    return 512 if points % 512 == 0 else BLOCK


def right_call(flags, xs, weights):
    rows, points = xs[0].shape
    rank = weights[0].shape[2]
    chunk = chunk_of(points)
    steps = points // chunk
    trace = pl.BlockSpec((rows, chunk), lambda i: (0, i))
    right = pl.BlockSpec((2, chunk, rank), lambda i: (0, i, 0))
    shape = (2, rows // 8, 8, BLOCK)
    return call(
        functools.partial(right_kernel, steps, len(xs)),
        (steps,),
        (flags, *xs, *weights),
        [SMEM, *[trace] * len(xs), right, right],
        fixed(*shape),
        f32(*shape),
        3 * 4 * rows * points * rank,
        [pltpu.VMEM((rows, rank), jnp.float32)],
    )


def far_call(flags, coefs, weights, bases, edges):
    rows, points = bases[0].shape
    rank = weights[0].shape[1]
    chunk = chunk_of(points)
    steps = points // chunk
    trace = pl.BlockSpec((rows, chunk), lambda i: (0, i))
    left = pl.BlockSpec((2, rank, chunk), lambda i: (0, 0, i))
    outs, shapes = [trace], [f32(rows, points)]
    if edges:
        outs, shapes = outs + [fixed(rows, BLOCK)] * 2, shapes + [f32(rows, BLOCK)] * 2
    return call(
        functools.partial(far_kernel, steps, len(coefs), len(bases) == 2),
        (steps,),
        (flags, *coefs, *weights, *bases),
        [SMEM, *[fixed(2, rows // 8, 8, BLOCK)] * len(coefs), *[left] * len(weights), *[trace] * len(bases)],
        outs,
        shapes,
        len(coefs) * 3 * 4 * rows * points * rank,
    )


def near_call(flags, x, before, after, local, weights, edges):
    rows, points = x.shape
    blocks, depth, width = weights[0].shape
    group = 4 if blocks % 4 == 0 else 1
    steps = blocks // group
    part = pl.BlockSpec((rows, group * BLOCK), lambda i: (0, i))
    near = pl.BlockSpec((group, depth, width), lambda i: (i, 0, 0))
    own = local is not None
    outs, shapes = [part], [f32(rows, points)]
    if edges:
        outs, shapes = outs + [fixed(rows, BLOCK)] * 2, shapes + [f32(rows, BLOCK)] * 2
    return call(
        functools.partial(near_kernel, steps, group, own, edges),
        (steps,),
        (flags, x, before, after, *([local] if own else []), *weights),
        [SMEM, fixed(rows, points), fixed(rows, BLOCK), fixed(rows, BLOCK), *([part] if own else []), near, near],
        outs,
        shapes,
        3 * 2 * rows * blocks * depth * width,
        [pltpu.VMEM((rows, points + 2 * BLOCK), jnp.bfloat16)] * 2,
    )


def split_left(x, factor):
    _, rank, points = x.shape
    part = pl.BlockSpec((1, rank, points), lambda i: (i, 0, 0))
    shapes = [jax.ShapeDtypeStruct(x.shape, jnp.bfloat16)] * 2
    if factor is None:
        return call(split_kernel, (2,), (x,), [part], [part] * 2, shapes)
    args = (x, factor.reshape(1, 1, points))
    return call(scale_kernel, (2,), args, [part, fixed(1, 1, points)], [part] * 2, shapes)


def split_near(x, factor):
    _, blocks, depth, width = x.shape
    group = 3 if blocks % 3 == 0 else 1
    ins = [
        pl.BlockSpec((2, group, depth, width), lambda i: (0, i, 0, 0)),
        pl.BlockSpec((group, 1, width), lambda i: (i, 0, 0)),
    ]
    out = pl.BlockSpec((group, depth, 2 * width), lambda i: (i, 0, 0))
    shapes = [jax.ShapeDtypeStruct((blocks, depth, 2 * width), jnp.bfloat16)] * 2
    return call(pair_kernel, (blocks // group,), (x, factor.reshape(blocks, 1, width)), ins, [out] * 2, shapes)


def on_device(slabs, tiles, local_field, material, contrast, low_left, low_right, near_blocks):
    _, sources, _, points = local_field.shape
    rank = low_left.shape[2]
    rows = 2 * sources
    slab, tile = lax.axis_index("slab"), lax.axis_index("tile")
    flags = jnp.stack([slab == 0, tile == 0, tile == tiles - 1, slab % 2 == 1]).astype(jnp.int32)

    def sent(x, target, across):
        pairs = [
            (s * tiles + t, target(s) * tiles + (t + across) % tiles) for s in range(slabs) for t in range(tiles)
        ]
        return lax.ppermute(x, AXES, pairs)

    def below(x, across=0):
        return sent(x, lambda s: (s + 1) % slabs, across)

    def partner(x, across=0):
        return sent(x, lambda s: s ^ 1, across)

    def beside(x, across):
        return sent(x, lambda s: s, across)

    def total(shares):
        pieces = shares.reshape(tiles, -1, BLOCK)
        parts = lax.all_to_all(pieces, "tile", 0, 0)
        whole = lambda n: fixed(*n.shape)
        copies = call(sum_kernel, (1,), (parts,), [whole(parts)], whole(parts), f32(*parts.shape))
        return lax.all_to_all(copies, "tile", 0, 0).reshape(shares.shape)

    local = local_field[:, :, 0].reshape(rows, points)
    first, last = local[:, :BLOCK], local[:, points - BLOCK :]
    factor = jnp.sum(
        jnp.where(material[0][None, :] == jnp.arange(contrast.shape[0], dtype=jnp.int32)[:, None], contrast[:, None], 0.0),
        axis=0,
    )
    right = split_left(low_right[0], None)
    left = split_left(low_left[0], factor)
    near = split_near(near_blocks[0], factor)

    w, w_first, w_last = local, first, last
    arrived = jnp.zeros_like(local)
    w_arrived = partner(w)
    shares = right_call(flags, (arrived, w_arrived), right)
    c = total(shares)
    v = near_call(flags, w_arrived, partner(w_last, 1), partner(w_first, -1), local, near, False)[0]
    t, first, last = far_call(flags, (c,), left, (w, v), True)

    upper_flat = (partner(low_left[0]) * partner(factor)).reshape(2 * rank, points)
    m = total(right_call(flags, (upper_flat,), right))
    u_before = beside(upper_flat[:, points - BLOCK :], 1)
    u_after = beside(upper_flat[:, :BLOCK], -1)
    q = near_call(flags, upper_flat, u_before, u_after, None, near, False)[0]
    g = far_call(flags, (m,), left, (q,), False)[0]
    through = split_left(g.reshape(2, rank, points), None)

    for _ in range(1, slabs // 2):
        arrived = below(t)
        w, w_first, w_last = near_call(flags, arrived, below(last, 1), below(first, -1), local, near, True)
        w_arrived = partner(w)
        c = total(right_call(flags, (arrived, w_arrived), right))
        v = near_call(flags, w_arrived, partner(w_last, 1), partner(w_first, -1), local, near, False)[0]
        t, first, last = far_call(flags, (c, partner(c)), (*left, *through), (w, v), True)
    return t.reshape(2, sources, 1, points)


def solution(mesh):
    slabs, tiles = mesh.shape["slab"], mesh.shape["tile"]
    return jax.shard_map(
        functools.partial(on_device, slabs, tiles),
        mesh=mesh,
        in_specs=(
            P(None, None, "slab", "tile"),
            P("slab", "tile"),
            P(),
            P("slab", None, None, "tile"),
            P("slab", None, "tile", None),
            P("slab", None, "tile", None, None),
        ),
        out_specs=P(None, None, "slab", "tile"),
        check_vma=False,
    )
```

```python
import functools
import jax
import jax.numpy as jnp
from jax import lax
from jax.experimental import pallas as pl
from jax.experimental.pallas import tpu as pltpu
from jax.sharding import PartitionSpec as P

AXES = ("slab", "tile")
BLOCK = 128
PARAMS = pltpu.CompilerParams(vmem_limit_bytes=24 * 1024 * 1024)
SMEM = pl.BlockSpec(memory_space=pltpu.SMEM)


def halves(x):
    high = x.astype(jnp.bfloat16)
    low = (x - high.astype(jnp.float32)).astype(jnp.bfloat16)
    return high, low


def dot(a, b):
    return jnp.dot(a, b, preferred_element_type=jnp.float32)


def split_dot(high, low, w_high, w_low):
    rows = high.shape[0]
    both = dot(jnp.concatenate([high, low], axis=0), w_high)
    return both[:rows] + both[rows:] + dot(high, w_low)


def complex_dot(high, low, wr_high, wr_low, wi_high, wi_low):
    with_real = split_dot(high, low, wr_high, wr_low)
    with_imag = split_dot(high, low, wi_high, wi_low)
    half = with_real.shape[0] // 2
    return jnp.concatenate(
        [
            with_real[:half] - with_imag[half:],
            with_imag[:half] + with_real[half:],
        ],
        axis=0,
    )


def at_step(step, body):
    pl.when(pl.program_id(0) == step)(body)


def store_edges(steps, part, first_ref, last_ref):
    def store_first():
        first_ref[...] = part[:, :BLOCK]

    def store_last():
        last_ref[...] = part[:, -BLOCK:]

    at_step(0, store_first)
    at_step(steps - 1, store_last)


def right_kernel(steps, count, flags, *refs):
    xs, (rh_ref, rl_ref, p_ref, acc) = refs[:count], refs[count:]
    x = jnp.where(flags[0] == 1, 0.0, xs[0][...])
    if count == 2:
        x = jnp.where(flags[3] == 1, xs[1][...], x)
    high, low = halves(x)
    share = complex_dot(high, low, rh_ref[0], rl_ref[0], rh_ref[1], rl_ref[1])

    def start():
        acc[...] = share

    def finish():
        whole = acc[...]
        half = p_ref.shape[0] // 2
        p_ref[:half] = whole[:, :BLOCK].reshape(half, 8, BLOCK)
        p_ref[half:] = whole[:, BLOCK:].reshape(half, 8, BLOCK)

    at_step(0, start)

    @pl.when(pl.program_id(0) > 0)
    def _():
        acc[...] += share

    at_step(steps - 1, finish)


def far_kernel(steps, count, flags, *refs):
    coefs, refs = refs[:count], refs[count:]
    weights, refs = refs[: 2 * count], refs[2 * count :]
    if count == 2:
        mh_ref, ml_ref, refs = refs[0], refs[1], refs[2:]
    even_ref, odd_ref, t_ref, first_ref, last_ref = refs[:5]
    scratch = refs[5:]

    def flat(c_ref):
        c = c_ref[...].reshape(2, -1, BLOCK)
        return jnp.concatenate([c[0], c[1]], axis=1)

    def load():
        c = flat(coefs[0])
        if count == 2:
            other = flat(coefs[1])
            high, low = halves(other)
            scratch[2][...], scratch[3][...] = high, low
            more = complex_dot(high, low, mh_ref[0], ml_ref[0], mh_ref[1], ml_ref[1])
            c = c + jnp.where(flags[3] == 1, more, 0.0)
        scratch[0][...], scratch[1][...] = halves(c)

    at_step(0, load)
    total = jnp.where(flags[3] == 1, odd_ref[...], even_ref[...])
    for k in range(count):
        high_ref, low_ref = weights[2 * k], weights[2 * k + 1]
        high, low = scratch[2 * k][...], scratch[2 * k + 1][...]
        more = complex_dot(high, low, high_ref[0], low_ref[0], high_ref[1], low_ref[1])
        if k == 1:
            more = jnp.where(flags[3] == 1, more, 0.0)
        total = total + more
    t_ref[...] = total
    store_edges(steps, total, first_ref, last_ref)


def through_kernel(m_ref, high_ref, low_ref):
    m = m_ref[...].reshape(2, -1, BLOCK)
    m = jnp.concatenate([m[0], m[1]], axis=1)
    high_ref[...], low_ref[...] = (part.reshape(high_ref.shape) for part in halves(m))


def near_kernel(steps, group, own, edges, flags, x_ref, before_ref, after_ref, *refs):
    if own:
        l_ref, refs = refs[0], refs[1:]
    nh_ref, nl_ref, w_ref = refs[:3]
    high, low = refs[-2:]
    points = x_ref.shape[1]

    def load():
        before = jnp.where(flags[1] == 1, 0.0, before_ref[...])
        after = jnp.where(flags[2] == 1, 0.0, after_ref[...])
        high[:, :BLOCK], low[:, :BLOCK] = halves(before)
        high[:, BLOCK : BLOCK + points], low[:, BLOCK : BLOCK + points] = halves(x_ref[...])
        high[:, BLOCK + points :], low[:, BLOCK + points :] = halves(after)

    at_step(0, load)
    parts = []
    for k in range(group):
        start = pl.multiple_of((pl.program_id(0) * group + k) * BLOCK, BLOCK)
        window = pl.ds(start, 3 * BLOCK)
        both = split_dot(high[:, window], low[:, window], nh_ref[k], nl_ref[k])
        half = both.shape[0] // 2
        part = jnp.concatenate(
            [
                both[:half, :BLOCK] - both[half:, BLOCK:],
                both[:half, BLOCK:] + both[half:, :BLOCK],
            ],
            axis=0,
        )
        here = slice(k * BLOCK, (k + 1) * BLOCK)
        if own:
            mine = l_ref[:, here]
            part = jnp.where(flags[0] == 1, mine, mine + part)
        w_ref[:, here] = part
        parts.append(part)
    if edges:

        def store_first():
            refs[3][...] = parts[0]

        def store_last():
            refs[4][...] = parts[-1]

        at_step(0, store_first)
        at_step(steps - 1, store_last)


def scale_kernel(x_ref, factor_ref, high_ref, low_ref):
    high_ref[...], low_ref[...] = halves(x_ref[...] * factor_ref[...])


def split_kernel(x_ref, high_ref, low_ref):
    high_ref[...], low_ref[...] = halves(x_ref[...])


def pair_kernel(x_ref, factor_ref, high_ref, low_ref):
    for k in range(2):
        here = slice(k * BLOCK, (k + 1) * BLOCK)
        high_ref[:, :, here], low_ref[:, :, here] = halves(x_ref[k] * factor_ref[...])


def sum_kernel(parts_ref, copies_ref):
    copies_ref[...] = jnp.broadcast_to(jnp.sum(parts_ref[...], axis=0)[None], copies_ref.shape)


def join_kernel(sum_first, first_ref, second_ref, joined_ref):
    depth = first_ref.shape[1]
    first, second = first_ref[...], second_ref[...]
    if sum_first:
        first = jnp.broadcast_to(jnp.sum(first, axis=0)[None], first.shape)
    else:
        second = jnp.broadcast_to(jnp.sum(second, axis=0)[None], second.shape)
    joined_ref[:, :depth] = first
    joined_ref[:, depth:] = second


def f32(*shape):
    return jax.ShapeDtypeStruct(shape, jnp.float32)


def call(body, grid, args, ins, outs, out_shape, flops=0, scratch=()):
    size = sum(a.size * a.dtype.itemsize for a in args)
    return pl.pallas_call(
        body,
        grid=grid,
        in_specs=ins,
        out_specs=outs,
        out_shape=out_shape,
        scratch_shapes=scratch,
        compiler_params=PARAMS,
        cost_estimate=pl.CostEstimate(flops=flops, bytes_accessed=size, transcendentals=0),
    )(*args)


def fixed(*shape):
    return pl.BlockSpec(shape, lambda i: (0,) * len(shape))


def chunk_of(points):
    return 512 if points % 512 == 0 else BLOCK


def right_call(flags, xs, weights):
    rows, points = xs[0].shape
    rank = weights[0].shape[2]
    chunk = chunk_of(points)
    steps = points // chunk
    trace = pl.BlockSpec((rows, chunk), lambda i: (0, i))
    right = pl.BlockSpec((2, chunk, rank), lambda i: (0, i, 0))
    shape = (rows // 4, 8, BLOCK)
    return call(
        functools.partial(right_kernel, steps, len(xs)),
        (steps,),
        (flags, *xs, *weights),
        [SMEM, *[trace] * len(xs), right, right],
        fixed(*shape),
        f32(*shape),
        3 * 4 * rows * points * rank,
        [pltpu.VMEM((rows, rank), jnp.float32)],
    )


def far_call(flags, coefs, weights, through, bases, place=0):
    rows, points = bases[0].shape
    rank = weights[0].shape[1]
    chunk = chunk_of(points)
    steps = points // chunk
    trace = pl.BlockSpec((rows, chunk), lambda i: (0, i))
    left = pl.BlockSpec((2, rank, chunk), lambda i: (0, 0, i))
    tiles = coefs[0].shape[0]
    shape = (tiles, 2 * rows // tiles, BLOCK)
    ins = [pl.BlockSpec(shape, lambda i, n=n: (0, n, 0)) for n in (place, 0)]
    return call(
        functools.partial(far_kernel, steps, len(coefs)),
        (steps,),
        (flags, *coefs, *weights, *through, *bases),
        [SMEM, *ins[: len(coefs)], *[left] * len(weights), *[fixed(2, rank, rank)] * len(through), trace, trace],
        [trace, fixed(rows, BLOCK), fixed(rows, BLOCK)],
        [f32(rows, points), f32(rows, BLOCK), f32(rows, BLOCK)],
        len(coefs) * 3 * 4 * rows * points * rank,
        [pltpu.VMEM((rows, rank), jnp.bfloat16)] * (2 * len(coefs)),
    )


def near_call(flags, x, before, after, local, weights, edges, place=0):
    rows, points = x.shape
    blocks, depth, width = weights[0].shape
    group = 4 if blocks % 4 == 0 else 1
    steps = blocks // group
    part = pl.BlockSpec((rows, group * BLOCK), lambda i: (0, i))
    near = pl.BlockSpec((group, depth, width), lambda i: (i, 0, 0))
    own = local is not None
    edge = pl.BlockSpec((rows, BLOCK), lambda i: (place, 0))
    outs, shapes = [part], [f32(rows, points)]
    if edges:
        outs, shapes = outs + [fixed(rows, BLOCK)] * 2, shapes + [f32(rows, BLOCK)] * 2
    return call(
        functools.partial(near_kernel, steps, group, own, edges),
        (steps,),
        (flags, x, before, after, *([local] if own else []), *weights),
        [SMEM, fixed(rows, points), edge, edge, *([part] if own else []), near, near],
        outs,
        shapes,
        3 * 2 * rows * blocks * depth * width,
        [pltpu.VMEM((rows, points + 2 * BLOCK), jnp.bfloat16)] * 2,
    )


def split_left(x, factor):
    _, rank, points = x.shape
    part = pl.BlockSpec((1, rank, points), lambda i: (i, 0, 0))
    shapes = [pltpu.VMEM(x.shape, jnp.bfloat16)] * 2
    if factor is None:
        return call(split_kernel, (2,), (x,), [part], [part] * 2, shapes)
    args = (x, factor.reshape(1, 1, points))
    return call(scale_kernel, (2,), args, [part, fixed(1, 1, points)], [part] * 2, shapes)


def split_near(x, factor):
    _, blocks, depth, width = x.shape
    group = 3 if blocks % 3 == 0 else 1
    ins = [
        pl.BlockSpec((2, group, depth, width), lambda i: (0, i, 0, 0)),
        pl.BlockSpec((group, 1, width), lambda i: (i, 0, 0)),
    ]
    out = pl.BlockSpec((group, depth, 2 * width), lambda i: (i, 0, 0))
    shapes = [pltpu.VMEM((blocks, depth, 2 * width), jnp.bfloat16)] * 2
    return call(pair_kernel, (blocks // group,), (x, factor.reshape(blocks, 1, width)), ins, [out] * 2, shapes)


def on_device(slabs, tiles, local_field, material, contrast, low_left, low_right, near_blocks):
    _, sources, _, points = local_field.shape
    rank = low_left.shape[2]
    rows = 2 * sources
    slab, tile = lax.axis_index("slab"), lax.axis_index("tile")
    flags = jnp.stack([slab == 0, tile == 0, tile == tiles - 1, slab % 2 == 1]).astype(jnp.int32)

    def sent(x, target, across):
        pairs = [
            (s * tiles + t, target(s) * tiles + (t + across) % tiles) for s in range(slabs) for t in range(tiles)
        ]
        return lax.ppermute(x, AXES, pairs)

    def below(x, across=0):
        return sent(x, lambda s: (s + 1) % slabs, across)

    def partner(x, across=0):
        return sent(x, lambda s: s ^ 1, across)

    def beside(x, across):
        return sent(x, lambda s: s, across)

    def exchanged(pieces):
        return lax.all_to_all(pieces, "tile", 0, 0)

    def repeated(parts, place=0):
        shape = (tiles, thin, BLOCK)
        part = pl.BlockSpec(shape, lambda i: (0, place, 0))
        return call(sum_kernel, (1,), (parts,), [part], fixed(*shape), f32(*shape))

    def joined(sum_first, first, second):
        shape = (tiles, thick + thin, BLOCK)
        body = functools.partial(join_kernel, sum_first)
        ins = [fixed(tiles, thick, BLOCK), fixed(tiles, thin, BLOCK)]
        return call(body, (1,), (first, second), ins, fixed(*shape), f32(*shape))

    def through_halves(both):
        part = pl.BlockSpec((tiles, thick, BLOCK), lambda i: (0, 0, 0))
        shapes = [pltpu.VMEM((2, rank, rank), jnp.bfloat16)] * 2
        return call(through_kernel, (1,), (both,), [part], [fixed(2, rank, rank)] * 2, shapes)

    thin = rows * rank // BLOCK // tiles
    thick = 2 * rank * rank // BLOCK // tiles

    local = local_field[:, :, 0].reshape(rows, points)
    first, last = local[:, :BLOCK], local[:, points - BLOCK :]
    factor = jnp.sum(
        jnp.where(material[0][None, :] == jnp.arange(contrast.shape[0], dtype=jnp.int32)[:, None], contrast[:, None], 0.0),
        axis=0,
    )
    tied = lax.optimization_barrier
    w_arrived = partner(local)
    lower, lower_factor = partner(low_left[0]), partner(factor)
    right = split_left(low_right[0], None)

    shares = right_call(flags, (w_arrived,), right)
    shares, lower, left_in, here = tied((shares, lower, low_left[0], local))
    parts = exchanged(shares)

    def edge(start):
        cut = slice(start, start + BLOCK)
        return jnp.concatenate([(left_in[:, :, cut] * factor[cut]).reshape(2 * rank, BLOCK), here[:, cut]], axis=0)

    before, after = partner(edge(points - BLOCK), 1), partner(edge(0), -1)
    upper = (lower * lower_factor).reshape(2 * rank, points)
    through_shares = right_call(flags, (upper,), right).reshape(tiles, thick, BLOCK)
    parts, through_shares, before, after = tied((parts, through_shares, before, after))
    pieces = joined(False, through_shares, parts)
    pieces, upper, before, after, w_arrived, near_in = tied(
        (pieces, upper, before, after, w_arrived, near_blocks[0])
    )
    both = exchanged(pieces)
    near = split_near(near_in, factor)
    v = near_call(flags, w_arrived, before, after, local, near, False, 2 * rank // rows)[0]
    both, v, upper, before, after, left_in = tied((both, v, upper, before, after, low_left[0]))
    left = split_left(left_in, factor)
    t, first, last = far_call(flags, (both,), left, (), (local, v), thick // thin)
    t, first, last, upper, upper_before, upper_after = tied((t, first, last, upper, before, after))

    for step in range(1, slabs // 2):
        arrived, before, after = below(t), below(last, 1), below(first, -1)
        if step == 1:
            q = near_call(flags, upper, upper_before, upper_after, None, near, False)[0]
            across = split_left(q.reshape(2, rank, points), None)
            before, after, across = tied((before, after, across))
        w, w_first, w_last = near_call(flags, arrived, before, after, local, near, True)
        w_arrived, w_before, w_after = partner(w), partner(w_last, 1), partner(w_first, -1)
        shares = right_call(flags, (arrived, w_arrived), right)
        if step == 1:
            shares = joined(True, both, shares)
            shares, across, w, w_arrived, w_before, w_after = tied((shares, across, w, w_arrived, w_before, w_after))
        else:
            shares, w, w_arrived, w_before, w_after = tied((shares, w, w_arrived, w_before, w_after))
        parts = exchanged(shares)
        copies = repeated(parts, thick // thin if step == 1 else 0)
        if step == 1:
            through = through_halves(parts)
            copies, through, w, w_arrived, w_before, w_after = tied((copies, through, w, w_arrived, w_before, w_after))
        else:
            copies, w, w_arrived, w_before, w_after = tied((copies, w, w_arrived, w_before, w_after))
        c = exchanged(copies)
        c, w, w_arrived, w_before, w_after = tied((c, w, w_arrived, w_before, w_after))
        v = near_call(flags, w_arrived, w_before, w_after, local, near, False)[0]
        t, first, last = far_call(flags, (c, partner(c)), (*left, *across), through, (w, v))
    return t.reshape(2, sources, 1, points)


def solution(mesh):
    slabs, tiles = mesh.shape["slab"], mesh.shape["tile"]
    return jax.shard_map(
        functools.partial(on_device, slabs, tiles),
        mesh=mesh,
        in_specs=(
            P(None, None, "slab", "tile"),
            P("slab", "tile"),
            P(),
            P("slab", None, None, "tile"),
            P("slab", None, "tile", None),
            P("slab", None, "tile", None, None),
        ),
        out_specs=P(None, None, "slab", "tile"),
        check_vma=False,
    )
```

```python
import functools
import jax
import jax.numpy as jnp
from jax import lax
from jax.experimental import pallas as pl
from jax.experimental.pallas import tpu as pltpu
from jax.sharding import PartitionSpec as P

AXES = ("slab", "tile")
BLOCK = 128
PARAMS = pltpu.CompilerParams(vmem_limit_bytes=24 * 1024 * 1024)
SMEM = pl.BlockSpec(memory_space=pltpu.SMEM)


def halves(x):
    high = x.astype(jnp.bfloat16)
    low = (x - high.astype(jnp.float32)).astype(jnp.bfloat16)
    return high, low


def dot(a, b):
    return jnp.dot(a, b, preferred_element_type=jnp.float32)


def split_dot(high, low, w_high, w_low):
    rows = high.shape[0]
    both = dot(jnp.concatenate([high, low], axis=0), w_high)
    return both[:rows] + both[rows:] + dot(high, w_low)


def complex_dot(high, low, wr_high, wr_low, wi_high, wi_low):
    with_real = split_dot(high, low, wr_high, wr_low)
    with_imag = split_dot(high, low, wi_high, wi_low)
    half = with_real.shape[0] // 2
    return jnp.concatenate(
        [
            with_real[:half] - with_imag[half:],
            with_imag[:half] + with_real[half:],
        ],
        axis=0,
    )


def at_step(step, body):
    pl.when(pl.program_id(0) == step)(body)


def right_kernel(steps, count, scaled, flags, *refs):
    xs, (rh_ref, rl_ref, p_ref, acc) = refs[:count], refs[-4:]
    x = jnp.where(flags[0] == 1, 0.0, xs[0][...])
    if scaled:
        x = x * refs[count][...]
    if count == 2:
        x = jnp.where(flags[3] == 1, xs[1][...], x)
    high, low = halves(x)
    share = complex_dot(high, low, rh_ref[0], rl_ref[0], rh_ref[1], rl_ref[1])

    def start():
        acc[...] = share

    def finish():
        whole = acc[...]
        half = p_ref.shape[0] // 2
        p_ref[:half] = whole[:, :BLOCK].reshape(half, 8, BLOCK)
        p_ref[half:] = whole[:, BLOCK:].reshape(half, 8, BLOCK)

    at_step(0, start)

    @pl.when(pl.program_id(0) > 0)
    def _():
        acc[...] += share

    at_step(steps - 1, finish)


def pieces_of(points):
    chunk = chunk_of(points)
    return [slice(i, i + chunk) for i in range(0, points, chunk)]


def share_kernel(count, flags, *refs):
    xs, (rh_ref, rl_ref, p_ref) = refs[:count], refs[count:]
    whole = None
    for here in pieces_of(xs[0].shape[1]):
        x = jnp.where(flags[0] == 1, 0.0, xs[0][:, here])
        if count == 2:
            x = jnp.where(flags[3] == 1, xs[1][:, here], x)
        high, low = halves(x)
        share = complex_dot(high, low, rh_ref[0, here], rl_ref[0, here], rh_ref[1, here], rl_ref[1, here])
        whole = share if whole is None else whole + share
    half = p_ref.shape[0] // 2
    p_ref[:half] = whole[:, :BLOCK].reshape(half, 8, BLOCK)
    p_ref[half:] = whole[:, BLOCK:].reshape(half, 8, BLOCK)


def far_kernel(count, place, flags, *refs):
    coefs, refs = refs[:count], refs[count:]
    weights, refs = refs[: 2 * count], refs[2 * count :]
    if count == 2:
        mh_ref, ml_ref, refs = refs[0], refs[1], refs[2:]
    even_ref, odd_ref, t_ref, first_ref, last_ref = refs
    depth = 2 * t_ref.shape[0] // coefs[0].shape[0]

    def flat(c):
        c = c.reshape(2, -1, BLOCK)
        return jnp.concatenate([c[0], c[1]], axis=1)

    c = flat(coefs[0][:, place * depth : (place + 1) * depth])
    parts = []
    if count == 2:
        high, low = halves(flat(coefs[1][...]))
        more = complex_dot(high, low, mh_ref[0], ml_ref[0], mh_ref[1], ml_ref[1])
        c = c + jnp.where(flags[3] == 1, more, 0.0)
        parts.append((high, low))
    parts.insert(0, halves(c))
    points = t_ref.shape[1]
    for here in pieces_of(points):
        total = jnp.where(flags[3] == 1, odd_ref[:, here], even_ref[:, here])
        for k, (high, low) in enumerate(parts):
            high_ref, low_ref = weights[2 * k], weights[2 * k + 1]
            more = complex_dot(
                high, low, high_ref[0, :, here], low_ref[0, :, here], high_ref[1, :, here], low_ref[1, :, here]
            )
            if k == 1:
                more = jnp.where(flags[3] == 1, more, 0.0)
            total = total + more
        t_ref[:, here] = total
        if here.start == 0:
            first_ref[...] = total[:, :BLOCK]
        if here.stop == points:
            last_ref[...] = total[:, -BLOCK:]


def through_kernel(m_ref, high_ref, low_ref):
    m = m_ref[...].reshape(2, -1, BLOCK)
    m = jnp.concatenate([m[0], m[1]], axis=1)
    high_ref[...], low_ref[...] = (part.reshape(high_ref.shape) for part in halves(m))


def near_kernel(steps, group, own, edges, scaled, flags, x_ref, before_ref, after_ref, *refs):
    if scaled:
        scale_ref, refs = refs[0], refs[1:]
    if own:
        l_ref, refs = refs[0], refs[1:]
    nh_ref, nl_ref, w_ref = refs[:3]
    high, low = refs[-2:]
    points = x_ref.shape[1]

    def load():
        before = jnp.where(flags[1] == 1, 0.0, before_ref[...])
        after = jnp.where(flags[2] == 1, 0.0, after_ref[...])
        high[:, :BLOCK], low[:, :BLOCK] = halves(before)
        x = x_ref[...] * scale_ref[...] if scaled else x_ref[...]
        high[:, BLOCK : BLOCK + points], low[:, BLOCK : BLOCK + points] = halves(x)
        high[:, BLOCK + points :], low[:, BLOCK + points :] = halves(after)

    at_step(0, load)
    parts = []
    for k in range(group):
        start = pl.multiple_of((pl.program_id(0) * group + k) * BLOCK, BLOCK)
        window = pl.ds(start, 3 * BLOCK)
        both = split_dot(high[:, window], low[:, window], nh_ref[k], nl_ref[k])
        half = both.shape[0] // 2
        part = jnp.concatenate(
            [
                both[:half, :BLOCK] - both[half:, BLOCK:],
                both[:half, BLOCK:] + both[half:, :BLOCK],
            ],
            axis=0,
        )
        here = slice(k * BLOCK, (k + 1) * BLOCK)
        if own:
            mine = l_ref[:, here]
            part = jnp.where(flags[0] == 1, mine, mine + part)
        w_ref[:, here] = part
        parts.append(part)
    if edges:

        def store_first():
            refs[3][...] = parts[0]

        def store_last():
            refs[4][...] = parts[-1]

        at_step(0, store_first)
        at_step(steps - 1, store_last)


def scale_kernel(x_ref, factor_ref, high_ref, low_ref):
    high_ref[...], low_ref[...] = halves(x_ref[...] * factor_ref[...])


def split_kernel(x_ref, high_ref, low_ref):
    high_ref[...], low_ref[...] = halves(x_ref[...])


def pair_kernel(x_ref, factor_ref, high_ref, low_ref):
    for k in range(2):
        here = slice(k * BLOCK, (k + 1) * BLOCK)
        high_ref[:, :, here], low_ref[:, :, here] = halves(x_ref[k] * factor_ref[...])


def sum_kernel(parts_ref, copies_ref):
    copies_ref[...] = jnp.broadcast_to(jnp.sum(parts_ref[...], axis=0)[None], copies_ref.shape)


def join_kernel(sum_first, first_ref, second_ref, joined_ref):
    depth = first_ref.shape[1]
    first, second = first_ref[...], second_ref[...]
    if sum_first:
        first = jnp.broadcast_to(jnp.sum(first, axis=0)[None], first.shape)
    else:
        second = jnp.broadcast_to(jnp.sum(second, axis=0)[None], second.shape)
    joined_ref[:, :depth] = first
    joined_ref[:, depth:] = second


def f32(*shape):
    return jax.ShapeDtypeStruct(shape, jnp.float32)


def call(body, grid, args, ins, outs, out_shape, flops=0, scratch=()):
    size = sum(a.size * a.dtype.itemsize for a in args)
    return pl.pallas_call(
        body,
        grid=grid,
        in_specs=ins,
        out_specs=outs,
        out_shape=out_shape,
        scratch_shapes=scratch,
        compiler_params=PARAMS,
        cost_estimate=pl.CostEstimate(flops=flops, bytes_accessed=size, transcendentals=0),
    )(*args)


def fixed(*shape):
    return pl.BlockSpec(shape, lambda i: (0,) * len(shape))


def chunk_of(points):
    return 512 if points % 512 == 0 else BLOCK


def right_call(flags, xs, weights, scale=None):
    rows, points = xs[0].shape
    rank = weights[0].shape[2]
    chunk = chunk_of(points)
    steps = points // chunk
    trace = pl.BlockSpec((rows, chunk), lambda i: (0, i))
    right = pl.BlockSpec((2, chunk, rank), lambda i: (0, i, 0))
    shape = (rows // 4, 8, BLOCK)
    return call(
        functools.partial(right_kernel, steps, len(xs), scale is not None),
        (steps,),
        (flags, *xs, *([] if scale is None else [scale]), *weights),
        [
            SMEM,
            *[trace] * len(xs),
            *([] if scale is None else [pl.BlockSpec((1, chunk), lambda i: (0, i))]),
            right,
            right,
        ],
        fixed(*shape),
        f32(*shape),
        3 * 4 * rows * points * rank,
        [pltpu.VMEM((rows, rank), jnp.float32)],
    )


def direct_call(body, args, shapes, flops):
    vmem = pl.BlockSpec(memory_space=pltpu.VMEM)
    return pl.pallas_call(
        body,
        in_specs=[SMEM] + [vmem] * (len(args) - 1),
        out_specs=[vmem] * len(shapes),
        out_shape=shapes,
        compiler_params=PARAMS,
        cost_estimate=pl.CostEstimate(flops=flops, bytes_accessed=flops // 64, transcendentals=0),
    )(*args)


def share_call(flags, xs, weights):
    rows, points = xs[0].shape
    rank = weights[0].shape[2]
    flops = 3 * 4 * rows * points * rank
    args = (flags, *xs, *weights)
    return direct_call(functools.partial(share_kernel, len(xs)), args, [f32(rows // 4, 8, BLOCK)], flops)[0]


def far_call(flags, coefs, weights, through, bases, place=0):
    rows, points = bases[0].shape
    rank = weights[0].shape[1]
    args = (flags, *coefs, *weights, *through, *bases)
    shapes = [f32(rows, points), f32(rows, BLOCK), f32(rows, BLOCK)]
    flops = len(coefs) * 3 * 4 * rows * points * rank
    return direct_call(functools.partial(far_kernel, len(coefs), place), args, shapes, flops)


def near_call(flags, x, before, after, local, weights, edges, place=0, scale=None):
    rows, points = x.shape
    blocks, depth, width = weights[0].shape
    group = 4 if blocks % 4 == 0 else 1
    steps = blocks // group
    part = pl.BlockSpec((rows, group * BLOCK), lambda i: (0, i))
    near = pl.BlockSpec((group, depth, width), lambda i: (i, 0, 0))
    own = local is not None
    edge = pl.BlockSpec((rows, BLOCK), lambda i: (place, 0))
    outs, shapes = [part], [f32(rows, points)]
    if edges:
        outs, shapes = outs + [fixed(rows, BLOCK)] * 2, shapes + [f32(rows, BLOCK)] * 2
    return call(
        functools.partial(near_kernel, steps, group, own, edges, scale is not None),
        (steps,),
        (flags, x, before, after, *([] if scale is None else [scale]), *([local] if own else []), *weights),
        [SMEM, fixed(rows, points), edge, edge, *([] if scale is None else [fixed(1, points)]), *([part] if own else []), near, near],
        outs,
        shapes,
        3 * 2 * rows * blocks * depth * width,
        [pltpu.VMEM((rows, points + 2 * BLOCK), jnp.bfloat16)] * 2,
    )


def split_left(x, factor, held=True):
    _, rank, points = x.shape
    part = pl.BlockSpec((1, rank, points), lambda i: (i, 0, 0))
    shapes = [(pltpu.VMEM if held else jax.ShapeDtypeStruct)(x.shape, jnp.bfloat16)] * 2
    if factor is None:
        return call(split_kernel, (2,), (x,), [part], [part] * 2, shapes)
    args = (x, factor.reshape(1, 1, points))
    return call(scale_kernel, (2,), args, [part, fixed(1, 1, points)], [part] * 2, shapes)


def split_near(x, factor):
    _, blocks, depth, width = x.shape
    group = 3 if blocks % 3 == 0 else 1
    ins = [
        pl.BlockSpec((2, group, depth, width), lambda i: (0, i, 0, 0)),
        pl.BlockSpec((group, 1, width), lambda i: (i, 0, 0)),
    ]
    out = pl.BlockSpec((group, depth, 2 * width), lambda i: (i, 0, 0))
    shapes = [pltpu.VMEM((blocks, depth, 2 * width), jnp.bfloat16)] * 2
    return call(pair_kernel, (blocks // group,), (x, factor.reshape(blocks, 1, width)), ins, [out] * 2, shapes)


def on_device(slabs, tiles, local_field, material, contrast, low_left, low_right, near_blocks):
    _, sources, _, points = local_field.shape
    rank = low_left.shape[2]
    rows = 2 * sources
    slab, tile = lax.axis_index("slab"), lax.axis_index("tile")
    flags = jnp.stack([slab == 0, tile == 0, tile == tiles - 1, slab % 2 == 1]).astype(jnp.int32)

    def sent(x, target, across):
        pairs = [
            (s * tiles + t, target(s) * tiles + (t + across) % tiles) for s in range(slabs) for t in range(tiles)
        ]
        return lax.ppermute(x, AXES, pairs)

    def below(x, across=0):
        return sent(x, lambda s: (s + 1) % slabs, across)

    def partner(x, across=0):
        return sent(x, lambda s: s ^ 1, across)

    def beside(x, across):
        return sent(x, lambda s: s, across)

    def exchanged(pieces):
        return lax.all_to_all(pieces, "tile", 0, 0)

    def repeated(parts, place=0):
        shape = (tiles, thin, BLOCK)
        part = pl.BlockSpec(shape, lambda i: (0, place, 0))
        return call(sum_kernel, (1,), (parts,), [part], fixed(*shape), f32(*shape))

    def joined(sum_first, first, second):
        shape = (tiles, thick + thin, BLOCK)
        body = functools.partial(join_kernel, sum_first)
        ins = [fixed(tiles, thick, BLOCK), fixed(tiles, thin, BLOCK)]
        return call(body, (1,), (first, second), ins, fixed(*shape), f32(*shape))

    def through_halves(both):
        part = pl.BlockSpec((tiles, thick, BLOCK), lambda i: (0, 0, 0))
        shapes = [pltpu.VMEM((2, rank, rank), jnp.bfloat16)] * 2
        return call(through_kernel, (1,), (both,), [part], [fixed(2, rank, rank)] * 2, shapes)

    thin = rows * rank // BLOCK // tiles
    thick = 2 * rank * rank // BLOCK // tiles

    local = local_field[:, :, 0].reshape(rows, points)
    first, last = local[:, :BLOCK], local[:, points - BLOCK :]
    factor = jnp.sum(
        jnp.where(material[0][None, :] == jnp.arange(contrast.shape[0], dtype=jnp.int32)[:, None], contrast[:, None], 0.0),
        axis=0,
    )
    tied = lax.optimization_barrier
    w_arrived = partner(local)
    lower, lower_factor = partner(low_left[0]), partner(factor)
    right = split_left(low_right[0], None)

    shares = share_call(flags, (w_arrived,), right)
    shares, lower, left_in, here = tied((shares, lower, low_left[0], local))
    parts = exchanged(shares)

    def edge(start):
        cut = slice(start, start + BLOCK)
        return jnp.concatenate([(left_in[:, :, cut] * factor[cut]).reshape(2 * rank, BLOCK), here[:, cut]], axis=0)

    before, after = partner(edge(points - BLOCK), 1), partner(edge(0), -1)
    upper, upper_scale = lower.reshape(2 * rank, points), lower_factor.reshape(1, points)
    through_shares = right_call(flags, (upper,), right, upper_scale).reshape(tiles, thick, BLOCK)
    parts, through_shares, before, after = tied((parts, through_shares, before, after))
    pieces = joined(False, through_shares, parts)
    pieces, upper, before, after, w_arrived, near_in = tied(
        (pieces, upper, before, after, w_arrived, near_blocks[0])
    )
    both = exchanged(pieces)
    near = split_near(near_in, factor)
    v = near_call(flags, w_arrived, before, after, local, near, False, 2 * rank // rows)[0]
    v, upper = tied((v, upper))
    q = near_call(flags, upper, before, after, None, near, False, 0, upper_scale)[0]
    across = split_left(q.reshape(2, rank, points), None, False)
    both, v, across, left_in = tied((both, v, across, low_left[0]))
    left = split_left(left_in, factor)
    t, first, last = far_call(flags, (both,), left, (), (local, v), thick // thin)

    for step in range(1, slabs // 2):
        arrived, before, after = below(t), below(last, 1), below(first, -1)
        w, w_first, w_last = near_call(flags, arrived, before, after, local, near, True)
        w_arrived, w_before, w_after = partner(w), partner(w_last, 1), partner(w_first, -1)
        shares = share_call(flags, (arrived, w_arrived), right)
        if step == 1:
            shares = joined(True, both, shares)
            shares, across, w, w_arrived, w_before, w_after = tied((shares, across, w, w_arrived, w_before, w_after))
        else:
            shares, w, w_arrived, w_before, w_after = tied((shares, w, w_arrived, w_before, w_after))
        parts = exchanged(shares)
        copies = repeated(parts, thick // thin if step == 1 else 0)
        if step == 1:
            through = through_halves(parts)
            copies, through, w, w_arrived, w_before, w_after = tied((copies, through, w, w_arrived, w_before, w_after))
        else:
            copies, w, w_arrived, w_before, w_after = tied((copies, w, w_arrived, w_before, w_after))
        c = exchanged(copies)
        c, w, w_arrived, w_before, w_after = tied((c, w, w_arrived, w_before, w_after))
        v = near_call(flags, w_arrived, w_before, w_after, local, near, False)[0]
        t, first, last = far_call(flags, (c, partner(c)), (*left, *across), through, (w, v))
    return t.reshape(2, sources, 1, points)


def solution(mesh):
    slabs, tiles = mesh.shape["slab"], mesh.shape["tile"]
    return jax.shard_map(
        functools.partial(on_device, slabs, tiles),
        mesh=mesh,
        in_specs=(
            P(None, None, "slab", "tile"),
            P("slab", "tile"),
            P(),
            P("slab", None, None, "tile"),
            P("slab", None, "tile", None),
            P("slab", None, "tile", None, None),
        ),
        out_specs=P(None, None, "slab", "tile"),
        check_vma=False,
    )
```

```python
import functools
import jax
import jax.numpy as jnp
from jax import lax
from jax.experimental import pallas as pl
from jax.experimental.pallas import tpu as pltpu
from jax.sharding import PartitionSpec as P

AXES = ("slab", "tile")
BLOCK = 128
PARAMS = pltpu.CompilerParams(vmem_limit_bytes=24 * 1024 * 1024)
SMEM = pl.BlockSpec(memory_space=pltpu.SMEM)


def halves(x):
    high = x.astype(jnp.bfloat16)
    low = (x - high.astype(jnp.float32)).astype(jnp.bfloat16)
    return high, low


def dot(a, b):
    return jnp.dot(a, b, preferred_element_type=jnp.float32)


def split_dot(high, low, w_high, w_low):
    rows = high.shape[0]
    both = dot(jnp.concatenate([high, low], axis=0), w_high)
    return both[:rows] + both[rows:] + dot(high, w_low)


def complex_dot(high, low, wr_high, wr_low, wi_high, wi_low):
    with_real = split_dot(high, low, wr_high, wr_low)
    with_imag = split_dot(high, low, wi_high, wi_low)
    half = with_real.shape[0] // 2
    return jnp.concatenate(
        [
            with_real[:half] - with_imag[half:],
            with_imag[:half] + with_real[half:],
        ],
        axis=0,
    )


def at_step(step, body):
    pl.when(pl.program_id(0) == step)(body)


def store_edges(steps, part, first_ref, last_ref):
    def store_first():
        first_ref[...] = part[:, :BLOCK]

    def store_last():
        last_ref[...] = part[:, -BLOCK:]

    at_step(0, store_first)
    at_step(steps - 1, store_last)


def right_kernel(steps, count, scaled, flags, *refs):
    xs, (rh_ref, rl_ref, p_ref, acc) = refs[:count], refs[-4:]
    x = jnp.where(flags[0] == 1, 0.0, xs[0][...])
    if scaled:
        x = x * refs[count][...]
    if count == 2:
        x = jnp.where(flags[3] == 1, xs[1][...], x)
    high, low = halves(x)
    share = complex_dot(high, low, rh_ref[0], rl_ref[0], rh_ref[1], rl_ref[1])

    def start():
        acc[...] = share

    def finish():
        whole = acc[...]
        half = p_ref.shape[0] // 2
        p_ref[:half] = whole[:, :BLOCK].reshape(half, 8, BLOCK)
        p_ref[half:] = whole[:, BLOCK:].reshape(half, 8, BLOCK)

    at_step(0, start)

    @pl.when(pl.program_id(0) > 0)
    def _():
        acc[...] += share

    at_step(steps - 1, finish)


def far_kernel(steps, count, flags, *refs):
    coefs, refs = refs[:count], refs[count:]
    weights, refs = refs[: 2 * count], refs[2 * count :]
    if count == 2:
        mh_ref, ml_ref, refs = refs[0], refs[1], refs[2:]
    even_ref, odd_ref, t_ref, first_ref, last_ref = refs[:5]
    scratch = refs[5:]

    def flat(c_ref):
        c = c_ref[...].reshape(2, -1, BLOCK)
        return jnp.concatenate([c[0], c[1]], axis=1)

    def load():
        c = flat(coefs[0])
        if count == 2:
            other = flat(coefs[1])
            high, low = halves(other)
            scratch[2][...], scratch[3][...] = high, low
            more = complex_dot(high, low, mh_ref[0], ml_ref[0], mh_ref[1], ml_ref[1])
            c = c + jnp.where(flags[3] == 1, more, 0.0)
        scratch[0][...], scratch[1][...] = halves(c)

    at_step(0, load)
    total = jnp.where(flags[3] == 1, odd_ref[...], even_ref[...])
    for k in range(count):
        high_ref, low_ref = weights[2 * k], weights[2 * k + 1]
        high, low = scratch[2 * k][...], scratch[2 * k + 1][...]
        more = complex_dot(high, low, high_ref[0], low_ref[0], high_ref[1], low_ref[1])
        if k == 1:
            more = jnp.where(flags[3] == 1, more, 0.0)
        total = total + more
    t_ref[...] = total
    store_edges(steps, total, first_ref, last_ref)


def through_kernel(m_ref, high_ref, low_ref):
    m = m_ref[...].reshape(2, -1, BLOCK)
    m = jnp.concatenate([m[0], m[1]], axis=1)
    high_ref[...], low_ref[...] = (part.reshape(high_ref.shape) for part in halves(m))


def near_kernel(steps, group, own, edges, scaled, flags, x_ref, before_ref, after_ref, *refs):
    if scaled:
        scale_ref, refs = refs[0], refs[1:]
    if own:
        l_ref, refs = refs[0], refs[1:]
    nh_ref, nl_ref, w_ref = refs[:3]
    high, low = refs[-2:]
    points = x_ref.shape[1]

    def load():
        before = jnp.where(flags[1] == 1, 0.0, before_ref[...])
        after = jnp.where(flags[2] == 1, 0.0, after_ref[...])
        high[:, :BLOCK], low[:, :BLOCK] = halves(before)
        x = x_ref[...] * scale_ref[...] if scaled else x_ref[...]
        high[:, BLOCK : BLOCK + points], low[:, BLOCK : BLOCK + points] = halves(x)
        high[:, BLOCK + points :], low[:, BLOCK + points :] = halves(after)

    at_step(0, load)
    parts = []
    for k in range(group):
        start = pl.multiple_of((pl.program_id(0) * group + k) * BLOCK, BLOCK)
        window = pl.ds(start, 3 * BLOCK)
        both = split_dot(high[:, window], low[:, window], nh_ref[k], nl_ref[k])
        half = both.shape[0] // 2
        part = jnp.concatenate(
            [
                both[:half, :BLOCK] - both[half:, BLOCK:],
                both[:half, BLOCK:] + both[half:, :BLOCK],
            ],
            axis=0,
        )
        here = slice(k * BLOCK, (k + 1) * BLOCK)
        if own:
            mine = l_ref[:, here]
            part = jnp.where(flags[0] == 1, mine, mine + part)
        w_ref[:, here] = part
        parts.append(part)
    if edges:

        def store_first():
            refs[3][...] = parts[0]

        def store_last():
            refs[4][...] = parts[-1]

        at_step(0, store_first)
        at_step(steps - 1, store_last)


def scale_kernel(x_ref, factor_ref, high_ref, low_ref):
    high_ref[...], low_ref[...] = halves(x_ref[...] * factor_ref[...])


def split_kernel(x_ref, high_ref, low_ref):
    high_ref[...], low_ref[...] = halves(x_ref[...])


def pair_kernel(x_ref, factor_ref, high_ref, low_ref):
    for k in range(2):
        here = slice(k * BLOCK, (k + 1) * BLOCK)
        high_ref[:, :, here], low_ref[:, :, here] = halves(x_ref[k] * factor_ref[...])


def sum_kernel(parts_ref, copies_ref):
    copies_ref[...] = jnp.broadcast_to(jnp.sum(parts_ref[...], axis=0)[None], copies_ref.shape)


def join_kernel(sum_first, first_ref, second_ref, joined_ref):
    depth = first_ref.shape[1]
    first, second = first_ref[...], second_ref[...]
    if sum_first:
        first = jnp.broadcast_to(jnp.sum(first, axis=0)[None], first.shape)
    else:
        second = jnp.broadcast_to(jnp.sum(second, axis=0)[None], second.shape)
    joined_ref[:, :depth] = first
    joined_ref[:, depth:] = second


def f32(*shape):
    return jax.ShapeDtypeStruct(shape, jnp.float32)


def call(body, grid, args, ins, outs, out_shape, flops=0, scratch=()):
    size = sum(a.size * a.dtype.itemsize for a in args)
    return pl.pallas_call(
        body,
        grid=grid,
        in_specs=ins,
        out_specs=outs,
        out_shape=out_shape,
        scratch_shapes=scratch,
        compiler_params=PARAMS,
        cost_estimate=pl.CostEstimate(flops=flops, bytes_accessed=size, transcendentals=0),
    )(*args)


def fixed(*shape):
    return pl.BlockSpec(shape, lambda i: (0,) * len(shape))


def chunk_of(points):
    return 512 if points % 512 == 0 else BLOCK


def right_call(flags, xs, weights, scale=None):
    rows, points = xs[0].shape
    rank = weights[0].shape[2]
    chunk = chunk_of(points)
    steps = points // chunk
    trace = pl.BlockSpec((rows, chunk), lambda i: (0, i))
    right = pl.BlockSpec((2, chunk, rank), lambda i: (0, i, 0))
    shape = (rows // 4, 8, BLOCK)
    return call(
        functools.partial(right_kernel, steps, len(xs), scale is not None),
        (steps,),
        (flags, *xs, *([] if scale is None else [scale]), *weights),
        [
            SMEM,
            *[trace] * len(xs),
            *([] if scale is None else [pl.BlockSpec((1, chunk), lambda i: (0, i))]),
            right,
            right,
        ],
        fixed(*shape),
        f32(*shape),
        3 * 4 * rows * points * rank,
        [pltpu.VMEM((rows, rank), jnp.float32)],
    )


def far_call(flags, coefs, weights, through, bases, place=0):
    rows, points = bases[0].shape
    rank = weights[0].shape[1]
    chunk = chunk_of(points)
    steps = points // chunk
    trace = pl.BlockSpec((rows, chunk), lambda i: (0, i))
    left = pl.BlockSpec((2, rank, chunk), lambda i: (0, 0, i))
    tiles = coefs[0].shape[0]
    shape = (tiles, 2 * rows // tiles, BLOCK)
    ins = [pl.BlockSpec(shape, lambda i, n=n: (0, n, 0)) for n in (place, 0)]
    return call(
        functools.partial(far_kernel, steps, len(coefs)),
        (steps,),
        (flags, *coefs, *weights, *through, *bases),
        [SMEM, *ins[: len(coefs)], *[left] * len(weights), *[fixed(2, rank, rank)] * len(through), trace, trace],
        [trace, fixed(rows, BLOCK), fixed(rows, BLOCK)],
        [f32(rows, points), f32(rows, BLOCK), f32(rows, BLOCK)],
        len(coefs) * 3 * 4 * rows * points * rank,
        [pltpu.VMEM((rows, rank), jnp.bfloat16)] * (2 * len(coefs)),
    )


def near_call(flags, x, before, after, local, weights, edges, place=0, scale=None):
    rows, points = x.shape
    blocks, depth, width = weights[0].shape
    group = 4 if blocks % 4 == 0 else 1
    steps = blocks // group
    part = pl.BlockSpec((rows, group * BLOCK), lambda i: (0, i))
    near = pl.BlockSpec((group, depth, width), lambda i: (i, 0, 0))
    own = local is not None
    edge = pl.BlockSpec((rows, BLOCK), lambda i: (place, 0))
    outs, shapes = [part], [f32(rows, points)]
    if edges:
        outs, shapes = outs + [fixed(rows, BLOCK)] * 2, shapes + [f32(rows, BLOCK)] * 2
    return call(
        functools.partial(near_kernel, steps, group, own, edges, scale is not None),
        (steps,),
        (flags, x, before, after, *([] if scale is None else [scale]), *([local] if own else []), *weights),
        [SMEM, fixed(rows, points), edge, edge, *([] if scale is None else [fixed(1, points)]), *([part] if own else []), near, near],
        outs,
        shapes,
        3 * 2 * rows * blocks * depth * width,
        [pltpu.VMEM((rows, points + 2 * BLOCK), jnp.bfloat16)] * 2,
    )


def split_left(x, factor, held=True):
    _, rank, points = x.shape
    part = pl.BlockSpec((1, rank, points), lambda i: (i, 0, 0))
    shapes = [(pltpu.VMEM if held else jax.ShapeDtypeStruct)(x.shape, jnp.bfloat16)] * 2
    if factor is None:
        return call(split_kernel, (2,), (x,), [part], [part] * 2, shapes)
    args = (x, factor.reshape(1, 1, points))
    return call(scale_kernel, (2,), args, [part, fixed(1, 1, points)], [part] * 2, shapes)


def split_near(x, factor):
    _, blocks, depth, width = x.shape
    group = 3 if blocks % 3 == 0 else 1
    ins = [
        pl.BlockSpec((2, group, depth, width), lambda i: (0, i, 0, 0)),
        pl.BlockSpec((group, 1, width), lambda i: (i, 0, 0)),
    ]
    out = pl.BlockSpec((group, depth, 2 * width), lambda i: (i, 0, 0))
    shapes = [pltpu.VMEM((blocks, depth, 2 * width), jnp.bfloat16)] * 2
    return call(pair_kernel, (blocks // group,), (x, factor.reshape(blocks, 1, width)), ins, [out] * 2, shapes)


def on_device(slabs, tiles, local_field, material, contrast, low_left, low_right, near_blocks):
    _, sources, _, points = local_field.shape
    rank = low_left.shape[2]
    rows = 2 * sources
    slab, tile = lax.axis_index("slab"), lax.axis_index("tile")
    flags = jnp.stack([slab == 0, tile == 0, tile == tiles - 1, slab % 2 == 1]).astype(jnp.int32)

    def sent(x, target, across):
        pairs = [
            (s * tiles + t, target(s) * tiles + (t + across) % tiles) for s in range(slabs) for t in range(tiles)
        ]
        return lax.ppermute(x, AXES, pairs)

    def below(x, across=0):
        return sent(x, lambda s: (s + 1) % slabs, across)

    def partner(x, across=0):
        return sent(x, lambda s: s ^ 1, across)

    def beside(x, across):
        return sent(x, lambda s: s, across)

    def exchanged(pieces):
        return lax.all_to_all(pieces, "tile", 0, 0)

    def repeated(parts, place=0):
        shape = (tiles, thin, BLOCK)
        part = pl.BlockSpec(shape, lambda i: (0, place, 0))
        return call(sum_kernel, (1,), (parts,), [part], fixed(*shape), f32(*shape))

    def joined(sum_first, first, second):
        shape = (tiles, thick + thin, BLOCK)
        body = functools.partial(join_kernel, sum_first)
        ins = [fixed(tiles, thick, BLOCK), fixed(tiles, thin, BLOCK)]
        return call(body, (1,), (first, second), ins, fixed(*shape), f32(*shape))

    def through_halves(both):
        part = pl.BlockSpec((tiles, thick, BLOCK), lambda i: (0, 0, 0))
        shapes = [pltpu.VMEM((2, rank, rank), jnp.bfloat16)] * 2
        return call(through_kernel, (1,), (both,), [part], [fixed(2, rank, rank)] * 2, shapes)

    thin = rows * rank // BLOCK // tiles
    thick = 2 * rank * rank // BLOCK // tiles

    local = local_field[:, :, 0].reshape(rows, points)
    first, last = local[:, :BLOCK], local[:, points - BLOCK :]
    factor = jnp.sum(
        jnp.where(material[0][None, :] == jnp.arange(contrast.shape[0], dtype=jnp.int32)[:, None], contrast[:, None], 0.0),
        axis=0,
    )
    tied = lax.optimization_barrier
    w_arrived = partner(local)
    lower, lower_factor = partner(low_left[0]), partner(factor)
    right = split_left(low_right[0], None)

    shares = right_call(flags, (w_arrived,), right)
    shares, lower, left_in, here = tied((shares, lower, low_left[0], local))
    parts = exchanged(shares)

    def edge(start):
        cut = slice(start, start + BLOCK)
        return jnp.concatenate([(left_in[:, :, cut] * factor[cut]).reshape(2 * rank, BLOCK), here[:, cut]], axis=0)

    before, after = partner(edge(points - BLOCK), 1), partner(edge(0), -1)
    upper, upper_scale = lower.reshape(2 * rank, points), lower_factor.reshape(1, points)
    through_shares = right_call(flags, (upper,), right, upper_scale).reshape(tiles, thick, BLOCK)
    parts, through_shares, before, after = tied((parts, through_shares, before, after))
    pieces = joined(False, through_shares, parts)
    pieces, upper, before, after, w_arrived, near_in = tied(
        (pieces, upper, before, after, w_arrived, near_blocks[0])
    )
    both = exchanged(pieces)
    near = split_near(near_in, factor)
    v = near_call(flags, w_arrived, before, after, local, near, False, 2 * rank // rows)[0]
    v, upper = tied((v, upper))
    q = near_call(flags, upper, before, after, None, near, False, 0, upper_scale)[0]
    across = split_left(q.reshape(2, rank, points), None, False)
    both, v, across, left_in = tied((both, v, across, low_left[0]))
    left = split_left(left_in, factor)
    t, first, last = far_call(flags, (both,), left, (), (local, v), thick // thin)

    for step in range(1, slabs // 2):
        arrived, before, after = below(t), below(last, 1), below(first, -1)
        w, w_first, w_last = near_call(flags, arrived, before, after, local, near, True)
        w_arrived, w_before, w_after = partner(w), partner(w_last, 1), partner(w_first, -1)
        shares = right_call(flags, (arrived, w_arrived), right)
        if step == 1:
            shares = joined(True, both, shares)
            shares, across, w, w_arrived, w_before, w_after = tied((shares, across, w, w_arrived, w_before, w_after))
        else:
            shares, w, w_arrived, w_before, w_after = tied((shares, w, w_arrived, w_before, w_after))
        parts = exchanged(shares)
        copies = repeated(parts, thick // thin if step == 1 else 0)
        if step == 1:
            through = through_halves(parts)
            copies, through, w, w_arrived, w_before, w_after = tied((copies, through, w, w_arrived, w_before, w_after))
        else:
            copies, w, w_arrived, w_before, w_after = tied((copies, w, w_arrived, w_before, w_after))
        c = exchanged(copies)
        c, w, w_arrived, w_before, w_after = tied((c, w, w_arrived, w_before, w_after))
        v = near_call(flags, w_arrived, w_before, w_after, local, near, False)[0]
        t, first, last = far_call(flags, (c, partner(c)), (*left, *across), through, (w, v))
    return t.reshape(2, sources, 1, points)


def solution(mesh):
    slabs, tiles = mesh.shape["slab"], mesh.shape["tile"]
    return jax.shard_map(
        functools.partial(on_device, slabs, tiles),
        mesh=mesh,
        in_specs=(
            P(None, None, "slab", "tile"),
            P("slab", "tile"),
            P(),
            P("slab", None, None, "tile"),
            P("slab", None, "tile", None),
            P("slab", None, "tile", None, None),
        ),
        out_specs=P(None, None, "slab", "tile"),
        check_vma=False,
    )
```
